32 devices in a mesh: ky: 8 (over y, x, core), kx: 4 (over z).
Axes of the slice: x: 2, y: 2, z: 4, core: 2. Of those that a mesh axis runs over, the one named last changes fastest.
Arguments:
- spectrum: bfloat16 [2, 4096, 2048], P(None, 'ky', 'kx'), may hold values from -6 to 6
- pupil_field: bfloat16 [2, 1024, 1024], replicated, may hold values from -3 to 3
- amplitude: bfloat16 [8192, 4096], P('ky', 'kx'), may hold values from 0 to 2
- offsets: int32 [8, 4, 2], P('ky', 'kx'), may hold values from -384 to 3456, as said below
Outputs:
- spectrum_grad: float32 [2, 4096, 2048], P(None, 'ky', 'kx')
- pupil_grad: float32 [2097152], P(('ky', 'kx'))
The draws below stay inside these ranges and needn't reach their ends.
Inputs may be any that keep to these rules, and one draw needn't show every extreme that they name: offsets[i, j] = (i * 512 - 512/2 + dy, j * 512 - 512/2 + dx) with whole numbers dy, dx from -128 to 128; both ends of this range are taken in every draw.
All inputs are finite; a program needn't handle non-finite values.
Results may differ from the reference program's by a relative error of at most 0.0028.
Values may be sent and summed in bfloat16 or wider, within the bound.
A program may use at most 192 MiB of HBM per device.

```python
import jax
import jax.numpy as jnp
from jax import lax

WIN = 1024
TILE = 512
SPEC_Y = 4096
SPEC_X = 2048
LEDS = 32
N_KY = 8
N_KX = 4


def draw_offsets(key, part):
    key = jax.random.fold_in(key, 11)
    subkeys = jax.random.split(key, 5)
    reach = TILE // 4
    jitter = jax.random.randint(subkeys[0], (N_KY, N_KX, 2), -reach, reach + 1).astype(jnp.int32)
    first_col = jax.random.randint(subkeys[1], (), 0, N_KX)
    second_col = jax.random.randint(subkeys[2], (), 0, N_KX)
    first_row = jax.random.randint(subkeys[3], (), 0, N_KY)
    second_row = jax.random.randint(subkeys[4], (), 0, N_KY)
    jitter = jitter.at[0, first_col, 0].set(-reach)
    jitter = jitter.at[N_KY - 1, second_col, 0].set(reach)
    jitter = jitter.at[first_row, 0, 1].set(-reach)
    jitter = jitter.at[second_row, N_KX - 1, 1].set(reach)
    row_base = jnp.arange(N_KY, dtype=jnp.int32)[:, None] * TILE - TILE // 2
    col_base = jnp.arange(N_KX, dtype=jnp.int32)[None, :] * TILE - TILE // 2
    row_part = row_base + jitter[:, :, 0]
    col_part = col_base + jitter[:, :, 1]
    return jnp.stack([row_part, col_part], axis=-1).astype(jnp.int32)


def levels(stream_key, dims, cuts, least, largest):
    loudness, own = 1.0, jax.random.fold_in(stream_key, 6)
    for dim, parts in cuts:
        draws = jnp.exp(jax.random.uniform(jax.random.fold_in(own, dim), (parts,), jnp.float32, least / len(cuts), largest / len(cuts)))
        loudness = loudness * jnp.repeat(draws, dims[dim] // parts).reshape([-1 if axis == dim else 1 for axis in range(len(dims))])
    return loudness


def normal_values(rng, dims, width, bound, cuts=(), kind=jnp.bfloat16):
    values = jax.random.normal(rng, dims, jnp.float32) * width
    if len(cuts) > 0:
        values = levels(rng, dims, cuts, -0.22, 0.18) * values
    return jnp.clip(values, min=-bound, max=bound).astype(kind)


def setup_inputs(seed: int = 0) -> dict:
    keys = jax.random.split(jax.random.key(seed), 5)
    spectrum = normal_values(keys[0], (2, SPEC_Y, SPEC_X), 1.0, 6.0, ((1, 8), (2, 4)))
    pupil_field = normal_values(keys[1], (2, WIN, WIN), 0.5, 3.0)
    amplitude = jnp.clip(2.0 * jax.random.uniform(keys[2], (WIN * N_KY, WIN * N_KX), jnp.float32) ** levels(keys[2], (WIN * N_KY, WIN * N_KX), ((0, 8), (1, 4)), -0.2, 0.2), 0.0, 2.0).astype(jnp.bfloat16)
    offsets = draw_offsets(jax.random.fold_in(keys[4], 71), 0)
    return dict(spectrum=spectrum, pupil_field=pupil_field, amplitude=amplitude, offsets=offsets)


AMP_FLOOR = 0.25


def reference(spectrum, pupil_field, amplitude, offsets):
    padding = TILE
    padded = jnp.pad(spectrum, ((0, 0), (padding, padding), (padding, padding)))
    pupil_complex = lax.complex(pupil_field[0].astype(jnp.float32), pupil_field[1].astype(jnp.float32))

    def one_led(carried, led_index):
        spec_sum, pupil_sum = carried
        led_row = led_index // N_KX
        led_col = led_index % N_KX
        row_start = (offsets[led_row, led_col, 0] + padding).astype(jnp.int32)
        col_start = (offsets[led_row, led_col, 1] + padding).astype(jnp.int32)
        zero_index = jnp.zeros((), jnp.int32)
        window = lax.dynamic_slice(padded, (zero_index, row_start, col_start), (2, WIN, WIN)).astype(jnp.float32)
        window_complex = lax.complex(window[0], window[1])
        amp_block = lax.dynamic_slice(amplitude, ((led_row * WIN).astype(jnp.int32), (led_col * WIN).astype(jnp.int32)), (WIN, WIN)).astype(jnp.float32)
        image_field = jnp.fft.ifft2(pupil_complex * window_complex, norm="ortho")
        magnitude = jnp.abs(image_field)
        residual = image_field - amp_block * image_field / jnp.maximum(magnitude, AMP_FLOOR)
        spec_residual = jnp.fft.fft2(residual, norm="ortho")
        window_grad = jnp.conj(pupil_complex) * spec_residual
        rounded = lax.optimization_barrier(jnp.stack([jnp.real(window_grad), jnp.imag(window_grad)]).astype(jnp.bfloat16))
        current = lax.dynamic_slice(spec_sum, (zero_index, row_start, col_start), (2, WIN, WIN))
        spec_sum = lax.dynamic_update_slice(spec_sum, current + rounded.astype(spec_sum.dtype), (zero_index, row_start, col_start))
        pupil_term = jnp.conj(window_complex) * spec_residual
        pupil_sum = pupil_sum + jnp.stack([jnp.real(pupil_term), jnp.imag(pupil_term)])
        return (spec_sum, pupil_sum), None

    start_state = (jnp.zeros(padded.shape, jnp.float32), jnp.zeros((2, WIN, WIN), jnp.float32))
    (spec_sum, pupil_sum), unused = lax.scan(one_led, start_state, jnp.arange(LEDS, dtype=jnp.int32))
    spectrum_grad = spec_sum[:, padding:padding + SPEC_Y, padding:padding + SPEC_X]
    pupil_grad = (pupil_sum / LEDS).reshape(-1)
    return spectrum_grad, pupil_grad
```

```python
import functools
import math

import jax
import jax.numpy as jnp
import ml_dtypes
import numpy as np
from jax import lax
from jax.experimental import pallas as pl
from jax.experimental.pallas import tpu as pltpu
from jax.sharding import PartitionSpec as P

WIN = 1024
A, B = 8, 128
RB = 64
SUB = 16
HALF_ROOT = math.sqrt(0.5)
BF = jnp.bfloat16
F32 = jnp.float32


def make_tables():
    k = np.arange(B)
    ang = 2.0 * np.pi * (np.outer(k, k) % B) / B
    c, s = np.cos(ang) / 32.0, np.sin(ang) / 32.0
    out = []
    for sign in (1.0, -1.0):
        m = np.block([[c, sign * s], [-sign * s, c]])
        hi = m.astype(np.float32).astype(ml_dtypes.bfloat16)
        lo = (m - hi.astype(np.float64)).astype(np.float32).astype(ml_dtypes.bfloat16)
        out.append(np.concatenate([hi, hi, lo], axis=0))
    lane = np.stack(out)
    rows = np.ascontiguousarray(lane.transpose(0, 2, 1))
    ang = 2.0 * np.pi * np.outer(np.arange(A), k) / WIN
    tw = np.stack([np.cos(ang), np.sin(ang)]).astype(np.float32)
    tw_rows = np.ascontiguousarray(np.broadcast_to(tw[:, :, :, None], (2, A, B, 128)))
    return lane, rows, tw, tw_rows


def cadd(x, y):
    return (x[0] + y[0], x[1] + y[1])


def csub(x, y):
    return (x[0] - y[0], x[1] - y[1])


def turn(x, sign):
    return (-x[1], x[0]) if sign > 0 else (x[1], -x[0])


def dft4(x0, x1, x2, x3, sign):
    s, d = cadd(x0, x2), csub(x0, x2)
    t, u = cadd(x1, x3), turn(csub(x1, x3), sign)
    return [cadd(s, t), cadd(d, u), csub(s, t), csub(d, u)]


def dft8(x, sign):
    e = dft4(x[0], x[2], x[4], x[6], sign)
    o = dft4(x[1], x[3], x[5], x[7], sign)
    o1 = cadd(o[1], turn(o[1], sign))
    o1 = (o1[0] * HALF_ROOT, o1[1] * HALF_ROOT)
    o2 = turn(o[2], sign)
    o3 = csub(turn(o[3], sign), o[3])
    o3 = (o3[0] * HALF_ROOT, o3[1] * HALF_ROOT)
    o = [o[0], o1, o2, o3]
    return [cadd(e[k], o[k]) for k in range(4)] + [csub(e[k], o[k]) for k in range(4)]


def split(x):
    hi = x.astype(BF)
    return hi, (x - hi.astype(F32)).astype(BF)


def mul_tw(x, tr, ti, sign):
    if sign > 0:
        return (x[0] * tr - x[1] * ti, x[0] * ti + x[1] * tr)
    return (x[0] * tr + x[1] * ti, x[1] * tr - x[0] * ti)


def kernel(
    inv_leds, starts, region, pupil, amp, lane_t, row_t, tw, tw_rows,
    frame, term, win, fld, lhs, rhs, out_l, out_r, gs,
):
    side = region.shape[1]
    row0, col0 = starts[0], starts[1]
    n_blocks = WIN // RB
    n_sub = RB // SUB

    def pass1(i, carry):
        r0 = row0 + i * RB
        base = jnp.minimum((r0 // 16) * 16, side - RB - 16)
        rem = r0 - base
        rows = pl.ds(pl.multiple_of(i * RB, RB), RB)
        for q in range(2):
            x = region[q, pl.ds(pl.multiple_of(base, 16), RB + 16), :].astype(F32)
            x = pltpu.roll(x, RB + 16 - rem, 0)[:RB]
            x = pltpu.roll(x, side - col0, 1)[:, :WIN]
            win[q, rows, :] = x.astype(BF)
        for s in range(n_sub):
            r = pl.ds(pl.multiple_of(i * RB + s * SUB, SUB), SUB)
            xs = []
            for a in range(A):
                cols = pl.ds(a * B, B)
                pr, pi = pupil[0, r, cols].astype(F32), pupil[1, r, cols].astype(F32)
                wr, wi = win[0, r, cols].astype(F32), win[1, r, cols].astype(F32)
                xs.append((pr * wr - pi * wi, pr * wi + pi * wr))
            ys = dft8(xs, 1)
            for c in range(A):
                y = ys[c]
                if c > 0:
                    y = mul_tw(y, tw[0, c : c + 1, :], tw[1, c : c + 1, :], 1)
                o = pl.ds(c * RB + s * SUB, SUB)
                for q in range(2):
                    hi, lo = split(y[q])
                    lhs[o, q * B : (q + 1) * B] = hi
                    lhs[o, (2 + q) * B : (3 + q) * B] = lo
        out_l[...] = jnp.dot(lhs[...], lane_t[0, :512, :], preferred_element_type=F32) + jnp.dot(
            lhs[:, :256], lane_t[0, 512:, :], preferred_element_type=F32
        )
        for c in range(A):
            for q in range(2):
                fld[q, rows, c * B : (c + 1) * B] = out_l[c * RB : (c + 1) * RB, q * B : (q + 1) * B]
        return carry

    lax.fori_loop(0, n_blocks, pass1, 0)

    def pass2(j, carry):
        cols = pl.ds(pl.multiple_of(j * B, B), B)
        for s in range(B // SUB):
            xs = [
                tuple(fld[q, a * B + s * SUB : a * B + (s + 1) * SUB, cols] for q in range(2))
                for a in range(A)
            ]
            ys = dft8(xs, 1)
            sl = slice(s * SUB, (s + 1) * SUB)
            for c in range(A):
                y = ys[c]
                if c > 0:
                    y = mul_tw(y, tw_rows[0, c, sl, :], tw_rows[1, c, sl, :], 1)
                for q in range(2):
                    hi, lo = split(y[q])
                    rhs[q * B + s * SUB : q * B + (s + 1) * SUB, c * B : (c + 1) * B] = hi
                    rhs[(2 + q) * B + s * SUB : (2 + q) * B + (s + 1) * SUB, c * B : (c + 1) * B] = lo
        out_r[...] = jnp.dot(row_t[0, :, :512], rhs[...], preferred_element_type=F32) + jnp.dot(
            row_t[0, :, 512:], rhs[:256, :], preferred_element_type=F32
        )
        for c in range(A):
            cc = slice(c * B, (c + 1) * B)
            for s in range(B // SUB):
                sl = slice(s * SUB, (s + 1) * SUB)
                zr = out_r[sl, cc]
                zi = out_r[B + s * SUB : B + (s + 1) * SUB, cc]
                m = amp[c * B + s * SUB : c * B + (s + 1) * SUB, cols].astype(F32)
                g = 1.0 - m * lax.rsqrt(jnp.maximum(zr * zr + zi * zi, 0.0625))
                for q, z in enumerate((zr * g, zi * g)):
                    hi, lo = split(z)
                    rhs[q * B + s * SUB : q * B + (s + 1) * SUB, cc] = hi
                    rhs[(2 + q) * B + s * SUB : (2 + q) * B + (s + 1) * SUB, cc] = lo
        out_r[...] = jnp.dot(row_t[1, :, :512], rhs[...], preferred_element_type=F32) + jnp.dot(
            row_t[1, :, 512:], rhs[:256, :], preferred_element_type=F32
        )
        for s in range(B // SUB):
            sl = slice(s * SUB, (s + 1) * SUB)
            ys = []
            for c in range(A):
                cc = slice(c * B, (c + 1) * B)
                y = (out_r[sl, cc], out_r[B + s * SUB : B + (s + 1) * SUB, cc])
                if c > 0:
                    y = mul_tw(y, tw_rows[0, c, sl, :], tw_rows[1, c, sl, :], -1)
                ys.append(y)
            xs = dft8(ys, -1)
            for a in range(A):
                for q in range(2):
                    fld[q, a * B + s * SUB : a * B + (s + 1) * SUB, cols] = xs[a][q]
        return carry

    lax.fori_loop(0, WIN // B, pass2, 0)

    pad = side - WIN
    gs[:, :pad, :] = jnp.zeros((2, pad, side), BF)
    gs[:, pad + WIN :, :] = jnp.zeros((2, pad, side), BF)
    gs[:, pad : pad + WIN, WIN:] = jnp.zeros((2, WIN, pad), BF)

    def pass3(i, carry):
        rows = pl.ds(pl.multiple_of(i * RB, RB), RB)
        for c in range(A):
            for q in range(2):
                hi, lo = split(fld[q, rows, c * B : (c + 1) * B])
                lhs[c * RB : (c + 1) * RB, q * B : (q + 1) * B] = hi
                lhs[c * RB : (c + 1) * RB, (2 + q) * B : (3 + q) * B] = lo
        out_l[...] = jnp.dot(lhs[...], lane_t[1, :512, :], preferred_element_type=F32) + jnp.dot(
            lhs[:, :256], lane_t[1, 512:, :], preferred_element_type=F32
        )
        for s in range(n_sub):
            r = pl.ds(pl.multiple_of(i * RB + s * SUB, SUB), SUB)
            rg = pl.ds(pl.multiple_of(pad + i * RB + s * SUB, SUB), SUB)
            ys = []
            for c in range(A):
                o = slice(c * RB + s * SUB, c * RB + (s + 1) * SUB)
                y = (out_l[o, :B], out_l[o, B:])
                if c > 0:
                    y = mul_tw(y, tw[0, c : c + 1, :], tw[1, c : c + 1, :], -1)
                ys.append(y)
            xs = dft8(ys, -1)
            for a in range(A):
                cols = pl.ds(a * B, B)
                sr, si = xs[a]
                pr, pi = pupil[0, r, cols].astype(F32), pupil[1, r, cols].astype(F32)
                wr, wi = win[0, r, cols].astype(F32), win[1, r, cols].astype(F32)
                gs[0, rg, cols] = (pr * sr + pi * si).astype(BF)
                gs[1, rg, cols] = (pr * si - pi * sr).astype(BF)
                term[0, r, cols] = (wr * sr + wi * si) * inv_leds
                term[1, r, cols] = (wr * si - wi * sr) * inv_leds
        return carry

    lax.fori_loop(0, n_blocks, pass3, 0)

    def pass4(k, carry):
        r0 = k * RB + pad - row0
        base = jnp.minimum((r0 // 16) * 16, gs.shape[1] - RB - 16)
        rem = r0 - base
        for q in range(2):
            x = gs[q, pl.ds(pl.multiple_of(base, 16), RB + 16), :].astype(F32)
            x = pltpu.roll(x, RB + 16 - rem, 0)[:RB]
            x = pltpu.roll(x, col0, 1)
            frame[q, pl.ds(pl.multiple_of(k * RB, RB), RB), :] = x.astype(BF)
        return carry

    lax.fori_loop(0, side // RB, pass4, 0)


def compute(starts, region, pupil, amp, n_leds):
    side = region.shape[1]
    pad = side - WIN
    lane, rows, tw, tw_rows = make_tables()
    vm = pl.BlockSpec(memory_space=pltpu.VMEM)
    return pl.pallas_call(
        functools.partial(kernel, 1.0 / n_leds),
        out_shape=(
            jax.ShapeDtypeStruct((2, side, side), BF),
            jax.ShapeDtypeStruct((2, WIN, WIN), F32),
        ),
        in_specs=[pl.BlockSpec(memory_space=pltpu.SMEM)] + [vm] * 7,
        out_specs=(vm, vm),
        scratch_shapes=[
            pltpu.VMEM((2, WIN, WIN), BF),
            pltpu.VMEM((2, WIN, WIN), F32),
            pltpu.VMEM((A * RB, 512), BF),
            pltpu.VMEM((512, WIN), BF),
            pltpu.VMEM((A * RB, 256), F32),
            pltpu.VMEM((256, WIN), F32),
            pltpu.VMEM((2, WIN + 2 * pad, side), BF),
        ],
        compiler_params=pltpu.CompilerParams(vmem_limit_bytes=60 * 1024 * 1024),
        cost_estimate=pl.CostEstimate(flops=13_000_000_000, bytes_accessed=30_000_000, transcendentals=1_000_000),
    )(starts, region, pupil, amp, jnp.asarray(lane), jnp.asarray(rows), jnp.asarray(tw), jnp.asarray(tw_rows))


def shift(x, axis, step):
    n = lax.axis_size(axis)
    pairs = [(i, i + step) for i in range(n) if 0 <= i + step < n]
    return lax.ppermute(x, axis, pairs)


def gather_region(tile, rim):
    t = tile.shape[1]
    left = shift(tile[:, :, t - rim :], "kx", 1)
    right = shift(tile[:, :, :rim], "kx", -1)
    up = shift(tile[:, t - rim :, :], "ky", 1)
    down = shift(tile[:, :rim, :], "ky", -1)
    sides = jnp.concatenate([left, right], axis=2)
    up_s = shift(sides[:, t - rim :, :], "ky", 1)
    down_s = shift(sides[:, :rim, :], "ky", -1)
    top = jnp.concatenate([up_s[:, :, :rim], up, up_s[:, :, rim:]], axis=2)
    mid = jnp.concatenate([left, tile, right], axis=2)
    bottom = jnp.concatenate([down_s[:, :, :rim], down, down_s[:, :, rim:]], axis=2)
    return jnp.concatenate([top, mid, bottom], axis=1)


def fold_rows(mid, from_up, from_down, rim):
    t = mid.shape[1]
    gap = t - rim
    x = mid.astype(F32)
    x = x + jnp.pad(from_up.astype(F32), ((0, 0), (0, gap), (0, 0)))
    return x + jnp.pad(from_down.astype(F32), ((0, 0), (gap, 0), (0, 0)))


def scatter_frame(frame, t, rim):
    lo, hi = rim, rim + t
    sides = jnp.concatenate([frame[:, :, :lo], frame[:, :, hi:]], axis=2)
    from_down_s = shift(sides[:, :lo, :], "ky", -1)
    from_up_s = shift(sides[:, hi:, :], "ky", 1)
    from_down = shift(frame[:, :lo, lo:hi], "ky", -1)
    from_up = shift(frame[:, hi:, lo:hi], "ky", 1)
    sides = fold_rows(sides[:, lo:hi, :], from_up_s, from_down_s, rim).astype(BF)
    from_right = shift(sides[:, :, :rim], "kx", -1)
    from_left = shift(sides[:, :, rim:], "kx", 1)
    out = fold_rows(frame[:, lo:hi, lo:hi], from_up, from_down, rim)
    gap = t - rim
    out = out + jnp.pad(from_left.astype(F32), ((0, 0), (0, 0), (0, gap)))
    return out + jnp.pad(from_right.astype(F32), ((0, 0), (0, 0), (gap, 0)))


def halve(x, dim, axis, weight, dtype):
    n = lax.axis_size(axis)
    bit = (lax.axis_index(axis) // weight) % 2
    keep = lax.dynamic_index_in_dim(x, bit, dim, keepdims=False)
    send = lax.dynamic_index_in_dim(x, 1 - bit, dim, keepdims=False).astype(dtype)
    got = lax.ppermute(send, axis, [(i, i ^ weight) for i in range(n)])
    return keep + got.astype(F32)


def reduce_terms(term):
    n_ky, n_kx = lax.axis_size("ky"), lax.axis_size("kx")
    bits_y, bits_x = n_ky.bit_length() - 1, n_kx.bit_length() - 1
    rows = 2 * WIN // (n_ky * n_kx)
    half = rows // 2
    flat = term.reshape([2] * (bits_y + bits_x) + [rows, WIN])

    def chain(x, order):
        left = list(range(bits_y + bits_x))
        for step, b in enumerate(order):
            dim = left.index(b)
            left.remove(b)
            axis, weight = ("ky", 1 << (bits_y - 1 - b)) if b < bits_y else ("kx", 1 << (bits_y + bits_x - 1 - b))
            x = halve(x, dim, axis, weight, BF if 1 <= step <= 4 else F32)
        return x

    core = [bits_y - 1]
    y_bits = list(range(bits_y - 2, -1, -1))
    x_bits = list(range(bits_y + bits_x - 1, bits_y - 1, -1))
    first = chain(flat[..., :half, :], core + y_bits + x_bits)
    second = chain(flat[..., half:, :], core + y_bits[::-1] + x_bits)
    return jnp.concatenate([first, second], axis=0).reshape(-1)


def body(spectrum, pupil_field, amplitude, offsets):
    t = spectrum.shape[1]
    rim = 3 * t // 4
    row_start = offsets[0, 0, 0] - (lax.axis_index("ky") * t - rim)
    col_start = offsets[0, 0, 1] - (lax.axis_index("kx") * t - rim)
    starts = jnp.stack([row_start, col_start]).astype(jnp.int32)
    k = jnp.arange(WIN, dtype=jnp.int32)
    source = (k % B) * A + k // B
    pick = (source[:, None] == k[None, :]).astype(BF)
    amp = jnp.dot(pick, amplitude, preferred_element_type=F32).astype(BF)
    amp = jnp.dot(amp, pick.T, preferred_element_type=F32).astype(BF)
    region = gather_region(spectrum, rim)
    n_leds = lax.axis_size("ky") * lax.axis_size("kx")
    frame, term = compute(starts, region, pupil_field, amp, n_leds)
    pupil_grad = reduce_terms(term)
    spectrum_grad = scatter_frame(frame, t, rim)
    return (spectrum_grad, pupil_grad)


def solution(mesh):
    return jax.shard_map(
        body,
        mesh=mesh,
        in_specs=(P(None, "ky", "kx"), P(), P("ky", "kx"), P("ky", "kx", None)),
        out_specs=(P(None, "ky", "kx"), P(("ky", "kx"))),
        check_vma=False,
    )
```

```python
import functools
import math

import jax
import jax.numpy as jnp
import ml_dtypes
import numpy as np
from jax import lax
from jax.experimental import pallas as pl
from jax.experimental.pallas import tpu as pltpu
from jax.sharding import PartitionSpec as P

WIN = 1024
A, B = 8, 128
RB = 64
SUB = 16
HALF_ROOT = math.sqrt(0.5)
BF = jnp.bfloat16
F32 = jnp.float32


def make_tables():
    k = np.arange(B)
    ang = 2.0 * np.pi * (np.outer(k, k) % B) / B
    c, s = np.cos(ang) / 32.0, np.sin(ang) / 32.0
    out = []
    for sign in (1.0, -1.0):
        m = np.block([[c, sign * s], [-sign * s, c]])
        hi = m.astype(np.float32).astype(ml_dtypes.bfloat16)
        lo = (m - hi.astype(np.float64)).astype(np.float32).astype(ml_dtypes.bfloat16)
        out.append(np.concatenate([hi, hi, lo], axis=0))
    lane = np.stack(out)
    rows = np.ascontiguousarray(lane.transpose(0, 2, 1))
    ang = 2.0 * np.pi * np.outer(np.arange(A), k) / WIN
    tw = np.stack([np.cos(ang), np.sin(ang)]).astype(np.float32)
    tw_rows = np.ascontiguousarray(np.broadcast_to(tw[:, :, :, None], (2, A, B, 128)))
    return lane, rows, tw, tw_rows


def cadd(x, y):
    return (x[0] + y[0], x[1] + y[1])


def csub(x, y):
    return (x[0] - y[0], x[1] - y[1])


def turn(x, sign):
    return (-x[1], x[0]) if sign > 0 else (x[1], -x[0])


def dft4(x0, x1, x2, x3, sign):
    s, d = cadd(x0, x2), csub(x0, x2)
    t, u = cadd(x1, x3), turn(csub(x1, x3), sign)
    return [cadd(s, t), cadd(d, u), csub(s, t), csub(d, u)]


def dft8(x, sign):
    e = dft4(x[0], x[2], x[4], x[6], sign)
    o = dft4(x[1], x[3], x[5], x[7], sign)
    o1 = cadd(o[1], turn(o[1], sign))
    o1 = (o1[0] * HALF_ROOT, o1[1] * HALF_ROOT)
    o2 = turn(o[2], sign)
    o3 = csub(turn(o[3], sign), o[3])
    o3 = (o3[0] * HALF_ROOT, o3[1] * HALF_ROOT)
    o = [o[0], o1, o2, o3]
    return [cadd(e[k], o[k]) for k in range(4)] + [csub(e[k], o[k]) for k in range(4)]


def split(x):
    hi = x.astype(BF)
    return hi, (x - hi.astype(F32)).astype(BF)


def mul_tw(x, tr, ti, sign):
    if sign > 0:
        return (x[0] * tr - x[1] * ti, x[0] * ti + x[1] * tr)
    return (x[0] * tr + x[1] * ti, x[1] * tr - x[0] * ti)


def kernel(
    inv_leds, starts, region, pupil, amp, lane_t, row_t, tw, tw_rows,
    frame, term, win, fld, lhs, rhs, out_l, out_r, gs,
):
    side = region.shape[1]
    row0, col0 = starts[0], starts[1]
    n_blocks = WIN // RB
    n_sub = RB // SUB

    def pass1(i, carry):
        r0 = row0 + i * RB
        base = jnp.minimum((r0 // 16) * 16, side - RB - 16)
        rem = r0 - base
        rows = pl.ds(pl.multiple_of(i * RB, RB), RB)
        for q in range(2):
            x = region[q, pl.ds(pl.multiple_of(base, 16), RB + 16), :].astype(F32)
            x = pltpu.roll(x, RB + 16 - rem, 0)[:RB]
            x = pltpu.roll(x, side - col0, 1)[:, :WIN]
            win[q, rows, :] = x.astype(BF)
        for s in range(n_sub):
            r = pl.ds(pl.multiple_of(i * RB + s * SUB, SUB), SUB)
            xs = []
            for a in range(A):
                cols = pl.ds(a * B, B)
                pr, pi = pupil[0, r, cols].astype(F32), pupil[1, r, cols].astype(F32)
                wr, wi = win[0, r, cols].astype(F32), win[1, r, cols].astype(F32)
                xs.append((pr * wr - pi * wi, pr * wi + pi * wr))
            ys = dft8(xs, 1)
            for c in range(A):
                y = ys[c]
                if c > 0:
                    y = mul_tw(y, tw[0, c : c + 1, :], tw[1, c : c + 1, :], 1)
                o = pl.ds(c * RB + s * SUB, SUB)
                for q in range(2):
                    hi, lo = split(y[q])
                    lhs[o, q * B : (q + 1) * B] = hi
                    lhs[o, (2 + q) * B : (3 + q) * B] = lo
        out_l[...] = jnp.dot(lhs[...], lane_t[0, :512, :], preferred_element_type=F32) + jnp.dot(
            lhs[:, :256], lane_t[0, 512:, :], preferred_element_type=F32
        )
        for c in range(A):
            for q in range(2):
                fld[q, rows, c * B : (c + 1) * B] = out_l[c * RB : (c + 1) * RB, q * B : (q + 1) * B]
        return carry

    lax.fori_loop(0, n_blocks, pass1, 0)

    def pass2(j, carry):
        cols = pl.ds(pl.multiple_of(j * B, B), B)
        for s in range(B // SUB):
            xs = [
                tuple(fld[q, a * B + s * SUB : a * B + (s + 1) * SUB, cols] for q in range(2))
                for a in range(A)
            ]
            ys = dft8(xs, 1)
            sl = slice(s * SUB, (s + 1) * SUB)
            for c in range(A):
                y = ys[c]
                if c > 0:
                    y = mul_tw(y, tw_rows[0, c, sl, :], tw_rows[1, c, sl, :], 1)
                for q in range(2):
                    hi, lo = split(y[q])
                    rhs[q * B + s * SUB : q * B + (s + 1) * SUB, c * B : (c + 1) * B] = hi
                    rhs[(2 + q) * B + s * SUB : (2 + q) * B + (s + 1) * SUB, c * B : (c + 1) * B] = lo
        out_r[...] = jnp.dot(row_t[0, :, :512], rhs[...], preferred_element_type=F32) + jnp.dot(
            row_t[0, :, 512:], rhs[:256, :], preferred_element_type=F32
        )
        for c in range(A):
            cc = slice(c * B, (c + 1) * B)
            for s in range(B // SUB):
                sl = slice(s * SUB, (s + 1) * SUB)
                zr = out_r[sl, cc]
                zi = out_r[B + s * SUB : B + (s + 1) * SUB, cc]
                m = amp[c * B + s * SUB : c * B + (s + 1) * SUB, cols].astype(F32)
                g = 1.0 - m * lax.rsqrt(jnp.maximum(zr * zr + zi * zi, 0.0625))
                for q, z in enumerate((zr * g, zi * g)):
                    hi, lo = split(z)
                    rhs[q * B + s * SUB : q * B + (s + 1) * SUB, cc] = hi
                    rhs[(2 + q) * B + s * SUB : (2 + q) * B + (s + 1) * SUB, cc] = lo
        out_r[...] = jnp.dot(row_t[1, :, :512], rhs[...], preferred_element_type=F32) + jnp.dot(
            row_t[1, :, 512:], rhs[:256, :], preferred_element_type=F32
        )
        for s in range(B // SUB):
            sl = slice(s * SUB, (s + 1) * SUB)
            ys = []
            for c in range(A):
                cc = slice(c * B, (c + 1) * B)
                y = (out_r[sl, cc], out_r[B + s * SUB : B + (s + 1) * SUB, cc])
                if c > 0:
                    y = mul_tw(y, tw_rows[0, c, sl, :], tw_rows[1, c, sl, :], -1)
                ys.append(y)
            xs = dft8(ys, -1)
            for a in range(A):
                for q in range(2):
                    fld[q, a * B + s * SUB : a * B + (s + 1) * SUB, cols] = xs[a][q]
        return carry

    lax.fori_loop(0, WIN // B, pass2, 0)

    pad = side - WIN
    gs[:, :pad, :] = jnp.zeros((2, pad, side), BF)
    gs[:, pad + WIN :, :] = jnp.zeros((2, pad, side), BF)
    gs[:, pad : pad + WIN, WIN:] = jnp.zeros((2, WIN, pad), BF)

    def pass3(i, carry):
        rows = pl.ds(pl.multiple_of(i * RB, RB), RB)
        for c in range(A):
            for q in range(2):
                hi, lo = split(fld[q, rows, c * B : (c + 1) * B])
                lhs[c * RB : (c + 1) * RB, q * B : (q + 1) * B] = hi
                lhs[c * RB : (c + 1) * RB, (2 + q) * B : (3 + q) * B] = lo
        out_l[...] = jnp.dot(lhs[...], lane_t[1, :512, :], preferred_element_type=F32) + jnp.dot(
            lhs[:, :256], lane_t[1, 512:, :], preferred_element_type=F32
        )
        for s in range(n_sub):
            r = pl.ds(pl.multiple_of(i * RB + s * SUB, SUB), SUB)
            rg = pl.ds(pl.multiple_of(pad + i * RB + s * SUB, SUB), SUB)
            ys = []
            for c in range(A):
                o = slice(c * RB + s * SUB, c * RB + (s + 1) * SUB)
                y = (out_l[o, :B], out_l[o, B:])
                if c > 0:
                    y = mul_tw(y, tw[0, c : c + 1, :], tw[1, c : c + 1, :], -1)
                ys.append(y)
            xs = dft8(ys, -1)
            for a in range(A):
                cols = pl.ds(a * B, B)
                sr, si = xs[a]
                pr, pi = pupil[0, r, cols].astype(F32), pupil[1, r, cols].astype(F32)
                wr, wi = win[0, r, cols].astype(F32), win[1, r, cols].astype(F32)
                gs[0, rg, cols] = (pr * sr + pi * si).astype(BF)
                gs[1, rg, cols] = (pr * si - pi * sr).astype(BF)
                term[0, r, cols] = (wr * sr + wi * si) * inv_leds
                term[1, r, cols] = (wr * si - wi * sr) * inv_leds
        return carry

    lax.fori_loop(0, n_blocks, pass3, 0)

    def pass4(k, carry):
        r0 = k * RB + pad - row0
        base = jnp.minimum((r0 // 16) * 16, gs.shape[1] - RB - 16)
        rem = r0 - base
        for q in range(2):
            x = gs[q, pl.ds(pl.multiple_of(base, 16), RB + 16), :].astype(F32)
            x = pltpu.roll(x, RB + 16 - rem, 0)[:RB]
            x = pltpu.roll(x, col0, 1)
            frame[q, pl.ds(pl.multiple_of(k * RB, RB), RB), :] = x.astype(BF)
        return carry

    lax.fori_loop(0, side // RB, pass4, 0)


def compute(starts, region, pupil, amp, n_leds):
    side = region.shape[1]
    pad = side - WIN
    lane, rows, tw, tw_rows = make_tables()
    vm = pl.BlockSpec(memory_space=pltpu.VMEM)
    return pl.pallas_call(
        functools.partial(kernel, 1.0 / n_leds),
        out_shape=(
            jax.ShapeDtypeStruct((2, side, side), BF),
            jax.ShapeDtypeStruct((2, WIN, WIN), F32),
        ),
        in_specs=[pl.BlockSpec(memory_space=pltpu.SMEM)] + [vm] * 7,
        out_specs=(vm, vm),
        scratch_shapes=[
            pltpu.VMEM((2, WIN, WIN), BF),
            pltpu.VMEM((2, WIN, WIN), F32),
            pltpu.VMEM((A * RB, 512), BF),
            pltpu.VMEM((512, WIN), BF),
            pltpu.VMEM((A * RB, 256), F32),
            pltpu.VMEM((256, WIN), F32),
            pltpu.VMEM((2, WIN + 2 * pad, side), BF),
        ],
        compiler_params=pltpu.CompilerParams(vmem_limit_bytes=60 * 1024 * 1024),
        cost_estimate=pl.CostEstimate(flops=13_000_000_000, bytes_accessed=30_000_000, transcendentals=1_000_000),
    )(starts, region, pupil, amp, jnp.asarray(lane), jnp.asarray(rows), jnp.asarray(tw), jnp.asarray(tw_rows))


MESH = pl.DeviceIdType.MESH


def remote(src, dst, send, recv, where):
    return pltpu.make_async_remote_copy(
        src_ref=src, dst_ref=dst, send_sem=send, recv_sem=recv, device_id=where, device_id_type=MESH
    )


def greet(sides):
    barrier = pltpu.get_barrier_semaphore()
    count = jnp.int32(0)
    for cond, where in sides:
        @pl.when(cond)
        def _(where=where):
            pl.semaphore_signal(barrier, inc=1, device_id=where, device_id_type=MESH)
        count = count + jnp.where(cond, 1, 0)
    pl.semaphore_wait(barrier, count)


def halo_kernel(n_ky, n_kx, rim, tile, region, send, recv):
    t = tile.shape[1]
    ky, kx = lax.axis_index("ky"), lax.axis_index("kx")
    has = {"u": ky > 0, "d": ky < n_ky - 1, "l": kx > 0, "r": kx < n_kx - 1}
    dev = {"u": (ky - 1, kx), "d": (ky + 1, kx), "l": (ky, kx - 1), "r": (ky, kx + 1)}
    back = {"u": "d", "d": "u", "l": "r", "r": "l"}
    far = {"u": pl.ds(0, rim), "d": pl.ds(rim + t, rim), "l": pl.ds(0, rim), "r": pl.ds(rim + t, rim), "": pl.ds(rim, t)}
    near = {"u": pl.ds(0, rim), "l": pl.ds(0, rim), "d": pl.ds(t - rim, rim), "r": pl.ds(t - rim, rim)}
    greet([(has[k], dev[k]) for k in "udlr"])
    whole = pl.ds(0, t)

    def strip(q, k):
        i = q * 8 + "udlr".index(k)
        rows = near[k] if k in "ud" else whole
        cols = near[k] if k in "lr" else whole
        o = back[k]
        dst = region.at[q, far[o] if k in "ud" else far[""], far[o] if k in "lr" else far[""]]
        return remote(tile.at[q, rows, cols], dst, send.at[i], recv.at[i], dev[k])

    def corner(q, k, side):
        i = q * 8 + 4 + "ud".index(k) * 2 + "lr".index(side)
        rows = pl.ds(rim, rim) if k == "u" else pl.ds(t, rim)
        return remote(
            region.at[q, rows, far[side]], region.at[q, far[back[k]], far[side]], send.at[i], recv.at[i], dev[k]
        )

    for q in range(2):
        for k in "lrud":
            @pl.when(has[k])
            def _(q=q, k=k):
                strip(q, k).start()
    for q in range(2):
        region[q, rim : rim + t, rim : rim + t] = tile[q]
    for k in "udlr":
        @pl.when(jnp.logical_not(has[k]))
        def _(k=k):
            for q in range(2):
                if k in "ud":
                    region[q, far[k], :] = jnp.zeros((rim, region.shape[2]), region.dtype)
                else:
                    region[q, far[""], far[k]] = jnp.zeros((t, rim), region.dtype)
                    for v in "ud":
                        @pl.when(has[v])
                        def _(q=q, k=k, v=v):
                            region[q, far[v], far[k]] = jnp.zeros((rim, rim), region.dtype)
    for q in range(2):
        for side in "lr":
            @pl.when(has[side])
            def _(q=q, side=side):
                strip(q, back[side]).wait_recv()
                for k in "ud":
                    @pl.when(has[k])
                    def _(k=k):
                        corner(q, k, side).start()
    for q in range(2):
        for k in "ud":
            @pl.when(has[k])
            def _(q=q, k=k):
                strip(q, back[k]).wait_recv()
                for side in "lr":
                    @pl.when(has[side])
                    def _(side=side):
                        corner(q, back[k], side).wait_recv()
                        corner(q, k, side).wait_send()
        for k in "udlr":
            @pl.when(has[k])
            def _(q=q, k=k):
                strip(q, k).wait_send()


def gather_region(tile, rim):
    t = tile.shape[1]
    side = t + 2 * rim
    vm = pl.BlockSpec(memory_space=pltpu.VMEM)
    return pl.pallas_call(
        functools.partial(halo_kernel, lax.axis_size("ky"), lax.axis_size("kx"), rim),
        out_shape=jax.ShapeDtypeStruct((2, side, side), tile.dtype),
        in_specs=[vm],
        out_specs=vm,
        scratch_shapes=[pltpu.SemaphoreType.DMA((16,)), pltpu.SemaphoreType.DMA((16,))],
        compiler_params=pltpu.CompilerParams(
            collective_id=0, has_side_effects=True, vmem_limit_bytes=32 * 1024 * 1024
        ),
    )(tile)


def shift(x, axis, step):
    n = lax.axis_size(axis)
    pairs = [(i, i + step) for i in range(n) if 0 <= i + step < n]
    return lax.ppermute(x, axis, pairs)


def fold_rows(mid, from_up, from_down, rim):
    t = mid.shape[1]
    gap = t - rim
    x = mid.astype(F32)
    x = x + jnp.pad(from_up.astype(F32), ((0, 0), (0, gap), (0, 0)))
    return x + jnp.pad(from_down.astype(F32), ((0, 0), (gap, 0), (0, 0)))


def scatter_frame(frame, t, rim):
    lo, hi = rim, rim + t
    sides = jnp.concatenate([frame[:, :, :lo], frame[:, :, hi:]], axis=2)
    from_down_s = shift(sides[:, :lo, :], "ky", -1)
    from_up_s = shift(sides[:, hi:, :], "ky", 1)
    from_down = shift(frame[:, :lo, lo:hi], "ky", -1)
    from_up = shift(frame[:, hi:, lo:hi], "ky", 1)
    sides = fold_rows(sides[:, lo:hi, :], from_up_s, from_down_s, rim).astype(BF)
    from_right = shift(sides[:, :, :rim], "kx", -1)
    from_left = shift(sides[:, :, rim:], "kx", 1)
    out = fold_rows(frame[:, lo:hi, lo:hi], from_up, from_down, rim)
    gap = t - rim
    out = out + jnp.pad(from_left.astype(F32), ((0, 0), (0, 0), (0, gap)))
    return out + jnp.pad(from_right.astype(F32), ((0, 0), (0, 0), (gap, 0)))


def halve(x, dim, axis, weight, dtype):
    n = lax.axis_size(axis)
    bit = (lax.axis_index(axis) // weight) % 2
    keep = lax.dynamic_index_in_dim(x, bit, dim, keepdims=False)
    send = lax.dynamic_index_in_dim(x, 1 - bit, dim, keepdims=False).astype(dtype)
    got = lax.ppermute(send, axis, [(i, i ^ weight) for i in range(n)])
    return keep + got.astype(F32)


def reduce_terms(term):
    n_ky, n_kx = lax.axis_size("ky"), lax.axis_size("kx")
    bits_y, bits_x = n_ky.bit_length() - 1, n_kx.bit_length() - 1
    rows = 2 * WIN // (n_ky * n_kx)
    half = rows // 2
    flat = term.reshape([2] * (bits_y + bits_x) + [rows, WIN])

    def chain(x, order):
        left = list(range(bits_y + bits_x))
        for step, b in enumerate(order):
            dim = left.index(b)
            left.remove(b)
            axis, weight = ("ky", 1 << (bits_y - 1 - b)) if b < bits_y else ("kx", 1 << (bits_y + bits_x - 1 - b))
            x = halve(x, dim, axis, weight, BF if 1 <= step <= 4 else F32)
        return x

    core = [bits_y - 1]
    y_bits = list(range(bits_y - 2, -1, -1))
    x_bits = list(range(bits_y + bits_x - 1, bits_y - 1, -1))
    first = chain(flat[..., :half, :], core + y_bits + x_bits)
    second = chain(flat[..., half:, :], core + y_bits[::-1] + x_bits)
    return jnp.concatenate([first, second], axis=0).reshape(-1)


def body(spectrum, pupil_field, amplitude, offsets):
    t = spectrum.shape[1]
    rim = 3 * t // 4
    row_start = offsets[0, 0, 0] - (lax.axis_index("ky") * t - rim)
    col_start = offsets[0, 0, 1] - (lax.axis_index("kx") * t - rim)
    starts = jnp.stack([row_start, col_start]).astype(jnp.int32)
    k = jnp.arange(WIN, dtype=jnp.int32)
    source = (k % B) * A + k // B
    pick = (source[:, None] == k[None, :]).astype(BF)
    amp = jnp.dot(pick, amplitude, preferred_element_type=F32).astype(BF)
    amp = jnp.dot(amp, pick.T, preferred_element_type=F32).astype(BF)
    region = gather_region(spectrum, rim)
    n_leds = lax.axis_size("ky") * lax.axis_size("kx")
    frame, term = compute(starts, region, pupil_field, amp, n_leds)
    pupil_grad = reduce_terms(term)
    spectrum_grad = scatter_frame(frame, t, rim)
    return (spectrum_grad, pupil_grad)


def solution(mesh):
    return jax.shard_map(
        body,
        mesh=mesh,
        in_specs=(P(None, "ky", "kx"), P(), P("ky", "kx"), P("ky", "kx", None)),
        out_specs=(P(None, "ky", "kx"), P(("ky", "kx"))),
        check_vma=False,
    )
```

```python
import functools
import math

import jax
import jax.numpy as jnp
import ml_dtypes
import numpy as np
from jax import lax
from jax.experimental import pallas as pl
from jax.experimental.pallas import tpu as pltpu
from jax.sharding import PartitionSpec as P

WIN = 1024
A, B = 8, 128
RB = 64
SUB = 16
HALF_ROOT = math.sqrt(0.5)
BF = jnp.bfloat16
F32 = jnp.float32


def make_tables():
    k = np.arange(B)
    ang = 2.0 * np.pi * (np.outer(k, k) % B) / B
    c, s = np.cos(ang) / 32.0, np.sin(ang) / 32.0
    out = []
    for sign in (1.0, -1.0):
        m = np.block([[c, sign * s], [-sign * s, c]])
        hi = m.astype(np.float32).astype(ml_dtypes.bfloat16)
        lo = (m - hi.astype(np.float64)).astype(np.float32).astype(ml_dtypes.bfloat16)
        out.append(np.concatenate([hi, hi, lo], axis=0))
    lane = np.stack(out)
    rows = np.ascontiguousarray(lane.transpose(0, 2, 1))
    ang = 2.0 * np.pi * np.outer(np.arange(A), k) / WIN
    tw = np.stack([np.cos(ang), np.sin(ang)]).astype(np.float32)
    tw_rows = np.ascontiguousarray(np.broadcast_to(tw[:, :, :, None], (2, A, B, 128)))
    return lane, rows, tw, tw_rows


def cadd(x, y):
    return (x[0] + y[0], x[1] + y[1])


def csub(x, y):
    return (x[0] - y[0], x[1] - y[1])


def turn(x, sign):
    return (-x[1], x[0]) if sign > 0 else (x[1], -x[0])


def dft4(x0, x1, x2, x3, sign):
    s, d = cadd(x0, x2), csub(x0, x2)
    t, u = cadd(x1, x3), turn(csub(x1, x3), sign)
    return [cadd(s, t), cadd(d, u), csub(s, t), csub(d, u)]


def dft8(x, sign):
    e = dft4(x[0], x[2], x[4], x[6], sign)
    o = dft4(x[1], x[3], x[5], x[7], sign)
    o1 = cadd(o[1], turn(o[1], sign))
    o1 = (o1[0] * HALF_ROOT, o1[1] * HALF_ROOT)
    o2 = turn(o[2], sign)
    o3 = csub(turn(o[3], sign), o[3])
    o3 = (o3[0] * HALF_ROOT, o3[1] * HALF_ROOT)
    o = [o[0], o1, o2, o3]
    return [cadd(e[k], o[k]) for k in range(4)] + [csub(e[k], o[k]) for k in range(4)]


def split(x):
    hi = x.astype(BF)
    return hi, (x - hi.astype(F32)).astype(BF)


def mul_tw(x, tr, ti, sign):
    if sign > 0:
        return (x[0] * tr - x[1] * ti, x[0] * ti + x[1] * tr)
    return (x[0] * tr + x[1] * ti, x[1] * tr - x[0] * ti)


def kernel(
    inv_leds, starts, region, pupil, amp, lane_t, row_t, tw, tw_rows,
    frame, term, win, fld, lhs, rhs, out_l, out_r, gs,
):
    side = region.shape[1]
    row0, col0 = starts[0], starts[1]
    n_blocks = WIN // RB
    n_sub = RB // SUB

    def pass1(i, carry):
        r0 = row0 + i * RB
        base = jnp.minimum((r0 // 16) * 16, side - RB - 16)
        rem = r0 - base
        rows = pl.ds(pl.multiple_of(i * RB, RB), RB)
        for q in range(2):
            x = region[q, pl.ds(pl.multiple_of(base, 16), RB + 16), :].astype(F32)
            x = pltpu.roll(x, RB + 16 - rem, 0)[:RB]
            x = pltpu.roll(x, side - col0, 1)[:, :WIN]
            win[q, rows, :] = x.astype(BF)
        for s in range(n_sub):
            r = pl.ds(pl.multiple_of(i * RB + s * SUB, SUB), SUB)
            xs = []
            for a in range(A):
                cols = pl.ds(a * B, B)
                pr, pi = pupil[0, r, cols].astype(F32), pupil[1, r, cols].astype(F32)
                wr, wi = win[0, r, cols].astype(F32), win[1, r, cols].astype(F32)
                xs.append((pr * wr - pi * wi, pr * wi + pi * wr))
            ys = dft8(xs, 1)
            for c in range(A):
                y = ys[c]
                if c > 0:
                    y = mul_tw(y, tw[0, c : c + 1, :], tw[1, c : c + 1, :], 1)
                o = pl.ds(c * RB + s * SUB, SUB)
                for q in range(2):
                    hi, lo = split(y[q])
                    lhs[o, q * B : (q + 1) * B] = hi
                    lhs[o, (2 + q) * B : (3 + q) * B] = lo
        out_l[...] = jnp.dot(lhs[...], lane_t[0, :512, :], preferred_element_type=F32) + jnp.dot(
            lhs[:, :256], lane_t[0, 512:, :], preferred_element_type=F32
        )
        for c in range(A):
            for q in range(2):
                fld[q, rows, c * B : (c + 1) * B] = out_l[c * RB : (c + 1) * RB, q * B : (q + 1) * B]
        return carry

    lax.fori_loop(0, n_blocks, pass1, 0)

    def pass2(j, carry):
        cols = pl.ds(pl.multiple_of(j * B, B), B)
        for s in range(B // SUB):
            xs = [
                tuple(fld[q, a * B + s * SUB : a * B + (s + 1) * SUB, cols] for q in range(2))
                for a in range(A)
            ]
            ys = dft8(xs, 1)
            sl = slice(s * SUB, (s + 1) * SUB)
            for c in range(A):
                y = ys[c]
                if c > 0:
                    y = mul_tw(y, tw_rows[0, c, sl, :], tw_rows[1, c, sl, :], 1)
                for q in range(2):
                    hi, lo = split(y[q])
                    rhs[q * B + s * SUB : q * B + (s + 1) * SUB, c * B : (c + 1) * B] = hi
                    rhs[(2 + q) * B + s * SUB : (2 + q) * B + (s + 1) * SUB, c * B : (c + 1) * B] = lo
        out_r[...] = jnp.dot(row_t[0, :, :512], rhs[...], preferred_element_type=F32) + jnp.dot(
            row_t[0, :, 512:], rhs[:256, :], preferred_element_type=F32
        )
        for c in range(A):
            cc = slice(c * B, (c + 1) * B)
            for s in range(B // SUB):
                sl = slice(s * SUB, (s + 1) * SUB)
                zr = out_r[sl, cc]
                zi = out_r[B + s * SUB : B + (s + 1) * SUB, cc]
                m = amp[c * B + s * SUB : c * B + (s + 1) * SUB, cols].astype(F32)
                g = 1.0 - m * lax.rsqrt(jnp.maximum(zr * zr + zi * zi, 0.0625))
                for q, z in enumerate((zr * g, zi * g)):
                    hi, lo = split(z)
                    rhs[q * B + s * SUB : q * B + (s + 1) * SUB, cc] = hi
                    rhs[(2 + q) * B + s * SUB : (2 + q) * B + (s + 1) * SUB, cc] = lo
        out_r[...] = jnp.dot(row_t[1, :, :512], rhs[...], preferred_element_type=F32) + jnp.dot(
            row_t[1, :, 512:], rhs[:256, :], preferred_element_type=F32
        )
        for s in range(B // SUB):
            sl = slice(s * SUB, (s + 1) * SUB)
            ys = []
            for c in range(A):
                cc = slice(c * B, (c + 1) * B)
                y = (out_r[sl, cc], out_r[B + s * SUB : B + (s + 1) * SUB, cc])
                if c > 0:
                    y = mul_tw(y, tw_rows[0, c, sl, :], tw_rows[1, c, sl, :], -1)
                ys.append(y)
            xs = dft8(ys, -1)
            for a in range(A):
                for q in range(2):
                    fld[q, a * B + s * SUB : a * B + (s + 1) * SUB, cols] = xs[a][q]
        return carry

    lax.fori_loop(0, WIN // B, pass2, 0)

    pad = side - WIN
    gs[:, :pad, :] = jnp.zeros((2, pad, side), BF)
    gs[:, pad + WIN :, :] = jnp.zeros((2, pad, side), BF)
    gs[:, pad : pad + WIN, WIN:] = jnp.zeros((2, WIN, pad), BF)

    def pass3(i, carry):
        rows = pl.ds(pl.multiple_of(i * RB, RB), RB)
        for c in range(A):
            for q in range(2):
                hi, lo = split(fld[q, rows, c * B : (c + 1) * B])
                lhs[c * RB : (c + 1) * RB, q * B : (q + 1) * B] = hi
                lhs[c * RB : (c + 1) * RB, (2 + q) * B : (3 + q) * B] = lo
        out_l[...] = jnp.dot(lhs[...], lane_t[1, :512, :], preferred_element_type=F32) + jnp.dot(
            lhs[:, :256], lane_t[1, 512:, :], preferred_element_type=F32
        )
        for s in range(n_sub):
            r = pl.ds(pl.multiple_of(i * RB + s * SUB, SUB), SUB)
            rg = pl.ds(pl.multiple_of(pad + i * RB + s * SUB, SUB), SUB)
            ys = []
            for c in range(A):
                o = slice(c * RB + s * SUB, c * RB + (s + 1) * SUB)
                y = (out_l[o, :B], out_l[o, B:])
                if c > 0:
                    y = mul_tw(y, tw[0, c : c + 1, :], tw[1, c : c + 1, :], -1)
                ys.append(y)
            xs = dft8(ys, -1)
            for a in range(A):
                cols = pl.ds(a * B, B)
                sr, si = xs[a]
                pr, pi = pupil[0, r, cols].astype(F32), pupil[1, r, cols].astype(F32)
                wr, wi = win[0, r, cols].astype(F32), win[1, r, cols].astype(F32)
                gs[0, rg, cols] = (pr * sr + pi * si).astype(BF)
                gs[1, rg, cols] = (pr * si - pi * sr).astype(BF)
                term[0, r, cols] = (wr * sr + wi * si) * inv_leds
                term[1, r, cols] = (wr * si - wi * sr) * inv_leds
        return carry

    lax.fori_loop(0, n_blocks, pass3, 0)

    def pass4(k, carry):
        r0 = k * RB + pad - row0
        base = jnp.minimum((r0 // 16) * 16, gs.shape[1] - RB - 16)
        rem = r0 - base
        for q in range(2):
            x = gs[q, pl.ds(pl.multiple_of(base, 16), RB + 16), :].astype(F32)
            x = pltpu.roll(x, RB + 16 - rem, 0)[:RB]
            x = pltpu.roll(x, col0, 1)
            frame[q, pl.ds(pl.multiple_of(k * RB, RB), RB), :] = x.astype(BF)
        return carry

    lax.fori_loop(0, side // RB, pass4, 0)


def compute(starts, region, pupil, amp, n_leds):
    side = region.shape[1]
    pad = side - WIN
    lane, rows, tw, tw_rows = make_tables()
    vm = pl.BlockSpec(memory_space=pltpu.VMEM)
    return pl.pallas_call(
        functools.partial(kernel, 1.0 / n_leds),
        out_shape=(
            jax.ShapeDtypeStruct((2, side, side), BF),
            jax.ShapeDtypeStruct((2, WIN, WIN), F32),
        ),
        in_specs=[pl.BlockSpec(memory_space=pltpu.SMEM)] + [vm] * 7,
        out_specs=(vm, vm),
        scratch_shapes=[
            pltpu.VMEM((2, WIN, WIN), BF),
            pltpu.VMEM((2, WIN, WIN), F32),
            pltpu.VMEM((A * RB, 512), BF),
            pltpu.VMEM((512, WIN), BF),
            pltpu.VMEM((A * RB, 256), F32),
            pltpu.VMEM((256, WIN), F32),
            pltpu.VMEM((2, WIN + 2 * pad, side), BF),
        ],
        compiler_params=pltpu.CompilerParams(vmem_limit_bytes=60 * 1024 * 1024),
        cost_estimate=pl.CostEstimate(flops=13_000_000_000, bytes_accessed=30_000_000, transcendentals=1_000_000),
    )(starts, region, pupil, amp, jnp.asarray(lane), jnp.asarray(rows), jnp.asarray(tw), jnp.asarray(tw_rows))


MESH = pl.DeviceIdType.MESH


def remote(src, dst, send, recv, where):
    return pltpu.make_async_remote_copy(
        src_ref=src, dst_ref=dst, send_sem=send, recv_sem=recv, device_id=where, device_id_type=MESH
    )


def greet(sides):
    barrier = pltpu.get_barrier_semaphore()
    count = jnp.int32(0)
    for cond, where in sides:
        @pl.when(cond)
        def _(where=where):
            pl.semaphore_signal(barrier, inc=1, device_id=where, device_id_type=MESH)
        count = count + jnp.where(cond, 1, 0)
    pl.semaphore_wait(barrier, count)


def halo_kernel(n_ky, n_kx, rim, tile, region, send, recv):
    t = tile.shape[1]
    ky, kx = lax.axis_index("ky"), lax.axis_index("kx")
    has = {"u": ky > 0, "d": ky < n_ky - 1, "l": kx > 0, "r": kx < n_kx - 1}
    dev = {"u": (ky - 1, kx), "d": (ky + 1, kx), "l": (ky, kx - 1), "r": (ky, kx + 1)}
    back = {"u": "d", "d": "u", "l": "r", "r": "l"}
    far = {"u": pl.ds(0, rim), "d": pl.ds(rim + t, rim), "l": pl.ds(0, rim), "r": pl.ds(rim + t, rim), "": pl.ds(rim, t)}
    near = {"u": pl.ds(0, rim), "l": pl.ds(0, rim), "d": pl.ds(t - rim, rim), "r": pl.ds(t - rim, rim)}
    greet([(has[k], dev[k]) for k in "udlr"])
    whole = pl.ds(0, t)

    def strip(q, k):
        i = q * 8 + "udlr".index(k)
        rows = near[k] if k in "ud" else whole
        cols = near[k] if k in "lr" else whole
        o = back[k]
        dst = region.at[q, far[o] if k in "ud" else far[""], far[o] if k in "lr" else far[""]]
        return remote(tile.at[q, rows, cols], dst, send.at[i], recv.at[i], dev[k])

    def corner(q, k, side):
        i = q * 8 + 4 + "ud".index(k) * 2 + "lr".index(side)
        rows = pl.ds(rim, rim) if k == "u" else pl.ds(t, rim)
        return remote(
            region.at[q, rows, far[side]], region.at[q, far[back[k]], far[side]], send.at[i], recv.at[i], dev[k]
        )

    for q in range(2):
        for k in "lrud":
            @pl.when(has[k])
            def _(q=q, k=k):
                strip(q, k).start()
    for q in range(2):
        region[q, rim : rim + t, rim : rim + t] = tile[q]
    for k in "udlr":
        @pl.when(jnp.logical_not(has[k]))
        def _(k=k):
            for q in range(2):
                if k in "ud":
                    region[q, far[k], :] = jnp.zeros((rim, region.shape[2]), region.dtype)
                else:
                    region[q, far[""], far[k]] = jnp.zeros((t, rim), region.dtype)
                    for v in "ud":
                        @pl.when(has[v])
                        def _(q=q, k=k, v=v):
                            region[q, far[v], far[k]] = jnp.zeros((rim, rim), region.dtype)
    for q in range(2):
        for side in "lr":
            @pl.when(has[side])
            def _(q=q, side=side):
                strip(q, back[side]).wait_recv()
                for k in "ud":
                    @pl.when(has[k])
                    def _(k=k):
                        corner(q, k, side).start()
    for q in range(2):
        for k in "ud":
            @pl.when(has[k])
            def _(q=q, k=k):
                strip(q, back[k]).wait_recv()
                for side in "lr":
                    @pl.when(has[side])
                    def _(side=side):
                        corner(q, back[k], side).wait_recv()
                        corner(q, k, side).wait_send()
        for k in "udlr":
            @pl.when(has[k])
            def _(q=q, k=k):
                strip(q, k).wait_send()


def gather_region(tile, rim):
    t = tile.shape[1]
    side = t + 2 * rim
    vm = pl.BlockSpec(memory_space=pltpu.VMEM)
    return pl.pallas_call(
        functools.partial(halo_kernel, lax.axis_size("ky"), lax.axis_size("kx"), rim),
        out_shape=jax.ShapeDtypeStruct((2, side, side), tile.dtype),
        in_specs=[vm],
        out_specs=vm,
        scratch_shapes=[pltpu.SemaphoreType.DMA((16,)), pltpu.SemaphoreType.DMA((16,))],
        compiler_params=pltpu.CompilerParams(
            collective_id=0, has_side_effects=True, vmem_limit_bytes=32 * 1024 * 1024
        ),
    )(tile)


def shift(x, axis, step):
    n = lax.axis_size(axis)
    pairs = [(i, i + step) for i in range(n) if 0 <= i + step < n]
    return lax.ppermute(x, axis, pairs)


def fold_rows(mid, from_up, from_down, rim):
    t = mid.shape[1]
    gap = t - rim
    x = mid.astype(F32)
    x = x + jnp.pad(from_up.astype(F32), ((0, 0), (0, gap), (0, 0)))
    return x + jnp.pad(from_down.astype(F32), ((0, 0), (gap, 0), (0, 0)))


def scatter_frame(frame, t, rim):
    lo, hi = rim, rim + t
    sides = jnp.concatenate([frame[:, :, :lo], frame[:, :, hi:]], axis=2)
    from_down_s = shift(sides[:, :lo, :], "ky", -1)
    from_up_s = shift(sides[:, hi:, :], "ky", 1)
    from_down = shift(frame[:, :lo, lo:hi], "ky", -1)
    from_up = shift(frame[:, hi:, lo:hi], "ky", 1)
    sides = fold_rows(sides[:, lo:hi, :], from_up_s, from_down_s, rim).astype(BF)
    from_right = shift(sides[:, :, :rim], "kx", -1)
    from_left = shift(sides[:, :, rim:], "kx", 1)
    out = fold_rows(frame[:, lo:hi, lo:hi], from_up, from_down, rim)
    gap = t - rim
    out = out + jnp.pad(from_left.astype(F32), ((0, 0), (0, 0), (0, gap)))
    return out + jnp.pad(from_right.astype(F32), ((0, 0), (0, 0), (gap, 0)))


def halve(x, dim, axis, weight, dtype):
    n = lax.axis_size(axis)
    bit = (lax.axis_index(axis) // weight) % 2
    keep = lax.dynamic_index_in_dim(x, bit, dim, keepdims=False)
    send = lax.dynamic_index_in_dim(x, 1 - bit, dim, keepdims=False).astype(dtype)
    got = lax.ppermute(send, axis, [(i, i ^ weight) for i in range(n)])
    return keep + got.astype(F32)


def reduce_terms(term):
    n_ky, n_kx = lax.axis_size("ky"), lax.axis_size("kx")
    bits_y, bits_x = n_ky.bit_length() - 1, n_kx.bit_length() - 1
    rows = 2 * WIN // (n_ky * n_kx)
    half = rows // 2
    flat = term.reshape([2] * (bits_y + bits_x) + [rows, WIN])

    def chain(x, order):
        left = list(range(bits_y + bits_x))
        for step, b in enumerate(order):
            dim = left.index(b)
            left.remove(b)
            axis, weight = ("ky", 1 << (bits_y - 1 - b)) if b < bits_y else ("kx", 1 << (bits_y + bits_x - 1 - b))
            x = halve(x, dim, axis, weight, BF if 1 <= step <= 4 else F32)
        return x

    core = [bits_y - 1]
    y_bits = list(range(bits_y - 2, -1, -1))
    x_bits = list(range(bits_y + bits_x - 1, bits_y - 1, -1))
    first = chain(flat[..., :half, :], core + y_bits + x_bits)
    second = chain(flat[..., half:, :], core + y_bits[::-1] + x_bits)
    return jnp.concatenate([first, second], axis=0).reshape(-1)


def flip(v, weights):
    for w in weights:
        v = v + w * (1 - 2 * ((v // w) % 2))
    return v


def finish_kernel(
    n_ky, n_kx, rim, frame, term, grad, pupil,
    got, acc, out_buf, in_buf, ring_u, ring_d, sides, ring_l, ring_r,
    core_send, core_recv, red_send, red_recv, rim_send, rim_recv, side_send, side_recv,
):
    t = grad.shape[1]
    ky, kx = lax.axis_index("ky"), lax.axis_index("kx")
    pair, core = ky // 2, ky % 2
    half = term.shape[3] // 2
    bits_y = [("ky", 1 << k) for k in range((n_ky // 2).bit_length() - 1)]
    bits_x = [("kx", 1 << k) for k in range(n_kx.bit_length() - 1)]
    bits = bits_y + bits_x
    orders = [bits_y + bits_x, bits_y[::-1] + bits_x[::-1]]
    n_slots = 1 << len(bits)

    def slot_bits(d):
        return [b for i, b in enumerate(bits) if (d >> i) & 1]

    def stage_of(d, h):
        on = slot_bits(d)
        for s, b in enumerate(orders[h]):
            if b in on:
                return s
        return len(bits)

    has = {"u": ky > 0, "d": ky < n_ky - 1, "l": kx > 0, "r": kx < n_kx - 1}
    dev = {"u": (ky - 1, kx), "d": (ky + 1, kx), "l": (ky, kx - 1), "r": (ky, kx + 1)}
    back = {"u": "d", "d": "u", "l": "r", "r": "l"}
    mate = (flip(ky, [1]), kx)

    def peer(b):
        return (2 * flip(pair, [b[1]]) + core, kx) if b[0] == "ky" else (ky, flip(kx, [b[1]]))

    always = ky >= 0
    greet([(has[k], dev[k]) for k in "udlr"] + [(always, mate)] + [(always, peer(b)) for b in bits])

    def place(d):
        on = slot_bits(d)
        return flip(pair, [w for n, w in on if n == "ky"]), flip(kx, [w for n, w in on if n == "kx"])

    def core_copy(d):
        g, c = place(d)
        return remote(term.at[g, 1 - core, c], got.at[d], core_send.at[d], core_recv.at[d], mate)

    def red_copy(h, d):
        b = orders[h][stage_of(d, h)]
        i = h * n_slots + d
        return remote(out_buf.at[i], in_buf.at[i], red_send.at[i], red_recv.at[i], peer(b))

    cols = [pl.ds(0, rim), pl.ds(rim + t, rim), pl.ds(rim, t)]

    def rim_copy(q, k, p):
        i = q * 6 + "ud".index(k) * 3 + p
        rows = pl.ds(0, rim) if k == "u" else pl.ds(rim + t, rim)
        dst = ring_d if k == "u" else ring_u
        return remote(frame.at[q, rows, cols[p]], dst.at[q, :, cols[p]], rim_send.at[i], rim_recv.at[i], dev[k])

    def side_copy(q, k):
        i = q * 2 + "lr".index(k)
        dst = ring_r if k == "l" else ring_l
        return remote(sides.at[q, "lr".index(k)], dst.at[q], side_send.at[i], side_recv.at[i], dev[k])

    order = sorted(range(n_slots), key=lambda d: (stage_of(d, 0) + stage_of(d, 1), d))
    for d in order:
        core_copy(d).start()
    for q in range(2):
        for p in range(2):
            for k in "ud":
                @pl.when(has[k])
                def _(q=q, k=k, p=p):
                    rim_copy(q, k, p).start()
    for k, ring in (("u", ring_u), ("d", ring_d), ("l", ring_l), ("r", ring_r)):
        @pl.when(jnp.logical_not(has[k]))
        def _(ring=ring):
            ring[...] = jnp.zeros(ring.shape, ring.dtype)

    def push(h, d, value):
        i = h * n_slots + d
        if d == 0:
            return
        out_buf[i] = value.astype(BF)
        red_copy(h, d).start()

    for d in order:
        core_copy(d).wait_recv()
        g, c = place(d)
        for h in range(2):
            rows = pl.ds(h * half, half)
            x = term[g, core, c, rows, :] + got[d, rows, :]
            if stage_of(d, h) == 0:
                push(h, d, x)
            else:
                acc[h * n_slots + d] = x
    for q in range(2):
        for k in "ud":
            @pl.when(has[k])
            def _(q=q, k=k):
                rim_copy(q, k, 2).start()
    for q in range(2):
        for p in range(2):
            for k in "ud":
                @pl.when(has[k])
                def _(q=q, k=k, p=p):
                    rim_copy(q, back[k], p).wait_recv()
            k = "lr"[p]
            mid = rim - (t - rim)
            for lo, n in ((0, t - rim), (t - rim, mid), (rim, t - rim)):
                x = frame[q, rim + lo : rim + lo + n, cols[p]].astype(F32)
                if lo < rim:
                    x = x + ring_u[q, lo : lo + n, cols[p]].astype(F32)
                if lo >= t - rim:
                    x = x + ring_d[q, lo - (t - rim) : lo - (t - rim) + n, cols[p]].astype(F32)
                sides[q, p, lo : lo + n, :] = x.astype(BF)

            @pl.when(has[k])
            def _(q=q, k=k):
                side_copy(q, k).start()
    for s in range(len(bits)):
        for h in range(2):
            for d in order:
                b = orders[h][s]
                before = [bits.index(v) for v in orders[h][: s + 1]]
                if any((d >> i) & 1 for i in before):
                    continue
                i = h * n_slots + d
                src = d ^ (1 << bits.index(b))
                red_copy(h, src).wait_recv()
                x = acc[i] + in_buf[h * n_slots + src].astype(F32)
                if stage_of(d, h) == s + 1 and d != 0:
                    push(h, d, x)
                elif d != 0:
                    acc[i] = x
                elif s < len(bits) - 1:
                    acc[i] = x
                else:
                    pupil[pl.ds(h * half, half), :] = x
    gap = t - rim
    for q in range(2):
        for k in "ud":
            @pl.when(has[k])
            def _(q=q, k=k):
                rim_copy(q, back[k], 2).wait_recv()
        for lo, n in ((0, gap), (gap, rim - gap), (rim, gap)):
            x = frame[q, rim + lo : rim + lo + n, cols[2]].astype(F32)
            if lo < rim:
                x = x + ring_u[q, lo : lo + n, cols[2]].astype(F32)
            if lo >= gap:
                x = x + ring_d[q, lo - gap : lo - gap + n, cols[2]].astype(F32)
            grad[q, lo : lo + n, :] = x
        for k in "lr":
            @pl.when(has[k])
            def _(q=q, k=k):
                side_copy(q, back[k]).wait_recv()
        grad[q, :, :rim] += ring_l[q].astype(F32)
        grad[q, :, gap:] += ring_r[q].astype(F32)
    for d in range(n_slots):
        core_copy(d).wait_send()
        if d:
            for h in range(2):
                red_copy(h, d).wait_send()
    for q in range(2):
        for k in "ud":
            @pl.when(has[k])
            def _(q=q, k=k):
                for p in range(3):
                    rim_copy(q, k, p).wait_send()
        for k in "lr":
            @pl.when(has[k])
            def _(q=q, k=k):
                side_copy(q, k).wait_send()


def finish(frame, term, t, rim):
    n_ky, n_kx = lax.axis_size("ky"), lax.axis_size("kx")
    rows = 2 * WIN // (n_ky * n_kx)
    n_slots = n_ky * n_kx // 2
    side = frame.shape[1]
    vm = pl.BlockSpec(memory_space=pltpu.VMEM)
    dma = pltpu.SemaphoreType.DMA
    grad, pupil = pl.pallas_call(
        functools.partial(finish_kernel, n_ky, n_kx, rim),
        out_shape=(jax.ShapeDtypeStruct((2, t, t), F32), jax.ShapeDtypeStruct((rows, WIN), F32)),
        in_specs=[vm, vm],
        out_specs=(vm, vm),
        scratch_shapes=[
            pltpu.VMEM((n_slots, rows, WIN), F32),
            pltpu.VMEM((2 * n_slots, rows // 2, WIN), F32),
            pltpu.VMEM((2 * n_slots, rows // 2, WIN), BF),
            pltpu.VMEM((2 * n_slots, rows // 2, WIN), BF),
            pltpu.VMEM((2, rim, side), BF),
            pltpu.VMEM((2, rim, side), BF),
            pltpu.VMEM((2, 2, t, rim), BF),
            pltpu.VMEM((2, t, rim), BF),
            pltpu.VMEM((2, t, rim), BF),
            dma((n_slots,)), dma((n_slots,)),
            dma((2 * n_slots,)), dma((2 * n_slots,)),
            dma((12,)), dma((12,)),
            dma((4,)), dma((4,)),
        ],
        compiler_params=pltpu.CompilerParams(
            collective_id=1, has_side_effects=True, vmem_limit_bytes=60 * 1024 * 1024
        ),
    )(frame, term.reshape(n_ky // 2, 2, n_kx, rows, WIN))
    return grad, pupil.reshape(-1)


def body(spectrum, pupil_field, amplitude, offsets):
    t = spectrum.shape[1]
    rim = 3 * t // 4
    row_start = offsets[0, 0, 0] - (lax.axis_index("ky") * t - rim)
    col_start = offsets[0, 0, 1] - (lax.axis_index("kx") * t - rim)
    starts = jnp.stack([row_start, col_start]).astype(jnp.int32)
    k = jnp.arange(WIN, dtype=jnp.int32)
    source = (k % B) * A + k // B
    pick = (source[:, None] == k[None, :]).astype(BF)
    amp = jnp.dot(pick, amplitude, preferred_element_type=F32).astype(BF)
    amp = jnp.dot(amp, pick.T, preferred_element_type=F32).astype(BF)
    region = gather_region(spectrum, rim)
    n_leds = lax.axis_size("ky") * lax.axis_size("kx")
    frame, term = compute(starts, region, pupil_field, amp, n_leds)
    if n_leds == 32:
        return finish(frame, term, t, rim)
    return (scatter_frame(frame, t, rim), reduce_terms(term))


def solution(mesh):
    return jax.shard_map(
        body,
        mesh=mesh,
        in_specs=(P(None, "ky", "kx"), P(), P("ky", "kx"), P("ky", "kx", None)),
        out_specs=(P(None, "ky", "kx"), P(("ky", "kx"))),
        check_vma=False,
    )
```
